256 devices in a mesh: row: 16 (over y, x), col: 16 (over z, core).
Axes of the slice: x: 4, y: 4, z: 8, core: 2. Of those that a mesh axis runs over, the one named last changes fastest.
Arguments:
- ids: int32 [2048], replicated, may hold values from 0 to 31999, as said below
- alpha: bfloat16 [2048, 2048], P('col', 'row'), may hold values from 0.0099487305 to 1
- beta: bfloat16 [2048, 32768], P('row', 'col'), may hold values from 0.0099487305 to 1
- emission: bfloat16 [32000, 32768], P('row', 'col'), may hold values from 0.049804688 to 1
- transition: bfloat16 [2048, 32768], P('row', 'col'), may hold values from 0.001 to 30, as said below
Outputs:
- counts: float32 [2048, 32768], P('row', 'col')
- new_trans: bfloat16 [2048, 32768], P('row', 'col')
The draws below stay inside these ranges and needn't reach their ends.
Inputs may be any that keep to these rules, and one draw needn't show every extreme that they name: Split the rows into 16 aligned blocks of 128 rows and the ids into 16 ranges of 2000 consecutive values: every block holds exactly 8 ids of every range. `transition`: positive weights.
All inputs are finite; a program needn't handle non-finite values.
Results may differ from the reference program's by a relative error of at most 0.0023.
Values may be sent and summed in bfloat16 or wider, within the bound.
No kernel may reach another device: no remote copies, remote signals or barrier semaphores. Data moves between devices by JAX's collectives and lax.ppermute only.
A program may use at most 128 MiB of HBM per device.

```python
import math
import jax
import jax.numpy as jnp

STATES = 32768
SRC = 2048
VOCAB = 32000
TIMES = 2048
N_ROW = 16


def draw_ids(key, part):
    key = jax.random.fold_in(key, 11)
    key_owner, key_word = jax.random.split(key, 2)
    span = TIMES // N_ROW
    pattern = jnp.arange(span, dtype=jnp.int32) % N_ROW
    owner_keys = jax.random.split(key_owner, N_ROW)
    owners = jax.vmap(lambda k: jax.random.permutation(k, pattern))(owner_keys).reshape(TIMES)
    words = jax.random.randint(key_word, (TIMES,), 0, VOCAB // N_ROW, dtype=jnp.int32)
    return (owners * (VOCAB // N_ROW) + words).astype(jnp.int32)


def draw_transition(key, part):
    key = jax.random.fold_in(key, 7)
    key_base, key_row, key_col = jax.random.split(key, 3)
    base = jnp.exp(jax.random.uniform(key_base, (SRC, STATES), jnp.float32, math.log(0.1), 0.0))
    row_scale = jnp.exp(jax.random.uniform(key_row, (SRC, 1), jnp.float32, 0.0, math.log(10.0)))
    position = jnp.arange(STATES, dtype=jnp.float32)[None, :] / (STATES - 1)
    ramp = 1.0 + 2.0 * position
    col_scale = jnp.exp(jax.random.uniform(key_col, (1, STATES), jnp.float32, 0.0, math.log(10.0)))
    return (0.02 * base * row_scale * ramp * col_scale).astype(jnp.bfloat16)


def block_scale(stream_key, extent, cuts, low, top_value):
    def one(axis_at, shards_of):
        heights = jax.random.uniform(jax.random.fold_in(jax.random.fold_in(stream_key, 6), axis_at), (shards_of,), jnp.float32, low / len(cuts), top_value / len(cuts))
        return jnp.repeat(jnp.exp(heights), extent[axis_at] // shards_of).reshape((-1,) + (1,) * (len(extent) - axis_at - 1))

    gain = one(*cuts[0])
    for cut in cuts[1:]:
        gain = gain * one(*cut)
    return gain


def setup_inputs(seed: int = 0) -> dict:
    splits = jax.random.split(jax.random.key(seed), 6)
    ids = draw_ids(jax.random.fold_in(splits[5], 71), 0)
    alpha = jnp.clip(jnp.exp(math.log(1.0) - 4.61031033 * jax.random.uniform(splits[1], (TIMES, SRC), jnp.float32) ** block_scale(splits[1], (TIMES, SRC), ((0, 16), (1, 16)), -0.2, 0.2)), 0.0099487305, 1.0).astype(jnp.bfloat16)
    beta = jnp.clip(jnp.exp(math.log(1.0) - 4.61031033 * jax.random.uniform(splits[2], (TIMES, STATES), jnp.float32) ** block_scale(splits[2], (TIMES, STATES), ((0, 16), (1, 16)), -0.2, 0.2)), 0.0099487305, 1.0).astype(jnp.bfloat16)
    emission = jnp.clip(jnp.exp(math.log(1.0) - 2.9996462 * jax.random.uniform(splits[3], (VOCAB, STATES), jnp.float32) ** block_scale(splits[3], (VOCAB, STATES), ((0, 16), (1, 16)), -0.2, 0.2)), 0.049804688, 1.0).astype(jnp.bfloat16)
    transition = draw_transition(jax.random.fold_in(splits[5], 71), 0)
    return {"ids": ids, "alpha": alpha, "beta": beta, "emission": emission, "transition": transition}


def reference(ids, alpha, beta, emission, transition):
    emitted = jnp.take(emission, ids, axis=0)
    scaled = (emitted.astype(jnp.float32) * beta.astype(jnp.float32)).astype(jnp.bfloat16)
    expected = jnp.dot(alpha.T, scaled, preferred_element_type=jnp.float32)
    counts = transition.astype(jnp.float32) * expected
    totals = jnp.sum(counts, axis=1)
    new_trans = (STATES * counts / totals[:, None]).astype(jnp.bfloat16)
    return counts, new_trans
```

```python
import jax
import jax.numpy as jnp
import numpy as np
from jax import lax
from jax.experimental import pallas as pl
from jax.experimental.pallas import tpu as pltpu
from jax.sharding import Mesh, PartitionSpec as P

STATES = 32768
RANGE = 2000
F32, BF16 = jnp.float32, jnp.bfloat16
VM = pl.BlockSpec(memory_space=pltpu.VMEM)
SM = pl.BlockSpec(memory_space=pltpu.SMEM)


def iota(shape, dim):
    return lax.broadcasted_iota(jnp.int32, shape, dim)


def params(mib):
    return pltpu.CompilerParams(vmem_limit_bytes=mib << 20)


def pick_kernel(pos, ids, table, out, hot):
    @pl.when(pl.program_id(0) == 0)
    def _():
        local = ids[...] - pos[0] * RANGE
        mine = (local >= 0) & (local < RANGE)
        upto = (iota((128, 128), 0) <= iota((128, 128), 1)).astype(BF16)
        count = jnp.dot(mine.astype(F32).astype(BF16), upto, preferred_element_type=F32)
        value = jnp.where(mine, local, 0).astype(F32)
        count = jnp.where(mine, count, 0.0)
        wide = lambda a: jnp.broadcast_to(a[:, None, :], (16, 8, 128)).reshape(128, 128)
        order = ((iota((128, 128), 0) & 7) + 1).astype(F32)
        word = jnp.sum(jnp.where(wide(count) == order, wide(value), 0.0), axis=1, keepdims=True)
        hot[...] = (iota((128, RANGE), 1) == word.astype(jnp.int32)).astype(F32).astype(BF16)

    rows = jnp.dot(hot[...], table[...], preferred_element_type=F32)
    out[...] = rows.astype(BF16).reshape(4, 1, 32, 512)


def pick(pos, ids, emission):
    return pl.pallas_call(
        pick_kernel,
        grid=(4,),
        in_specs=[SM, pl.BlockSpec((16, 128), lambda j: (0, 0)), pl.BlockSpec((RANGE, 512), lambda j: (0, j))],
        out_specs=pl.BlockSpec((4, 1, 32, 512), lambda j: (0, j, 0, 0)),
        out_shape=jax.ShapeDtypeStruct((4, 4, 32, 512), BF16),
        scratch_shapes=[pltpu.VMEM((128, RANGE), BF16)],
        compiler_params=params(32),
        name="pick",
    )(pos, ids, emission)


def scale_kernel(pos, ids, rows, b0, b1, b2, b3, out, wide):
    wide[...] = rows[...].astype(F32)
    before = (iota((128, 128), 0) < iota((128, 128), 1)).astype(BF16)
    for d, beta in enumerate((b0, b1, b2, b3)):
        block = (pos[2] - d + 4) & 3
        word = ids[pl.ds(pos[1] * 4 + block, 1), :]
        wordb = jnp.broadcast_to(word, (16, 128))
        owner_at = iota((16, 128), 0)
        owns = (wordb >= owner_at * RANGE) & (wordb < (owner_at + 1) * RANGE)
        ownf = owns.astype(F32)
        earlier = jnp.dot(ownf.astype(BF16), before, preferred_element_type=F32)
        place = ownf * (earlier + (owner_at * 8).astype(F32))
        slot = jnp.sum(place, axis=0, keepdims=True).astype(jnp.int32)
        move = (iota((128, 128), 0) == slot).astype(F32).astype(BF16)
        given = wide[:, pl.ds(pl.multiple_of(block * 8, 8), 8), :].reshape(128, 512).astype(BF16)
        emitted = lax.dot_general(move, given, (((0,), (0,)), ((), ())), preferred_element_type=F32)
        out[block] = (emitted * beta[...].astype(F32)).astype(BF16)


def scale(pos, ids, rows, betas):
    return pl.pallas_call(
        scale_kernel,
        in_specs=[SM] + [VM] * 6,
        out_specs=VM,
        out_shape=jax.ShapeDtypeStruct((4, 128, 512), BF16),
        scratch_shapes=[pltpu.VMEM((16, 32, 512), F32)],
        compiler_params=params(32),
        name="scale",
    )(pos, ids, rows, *betas)


def turn_kernel(alpha, out):
    for x in range(4):
        out[0, x * 128 : (x + 1) * 128, :] = alpha[x].T


def turn(alpha):
    return pl.pallas_call(
        turn_kernel,
        grid=(4,),
        in_specs=[pl.BlockSpec((4, 512, 128), lambda g: (0, g, 0))],
        out_specs=pl.BlockSpec((1, 512, 512), lambda g: (g, 0, 0)),
        out_shape=jax.ShapeDtypeStruct((4, 512, 512), BF16),
        compiler_params=params(32),
        name="turn",
    )(alpha)


def expect_kernel(pos, alpha, s0, s1, s2, s3, out):
    step = 1 - 2 * pos[3]
    groups = (pos[1], (pos[1] - step + 4) & 3, (pos[1] + step + 4) & 3, (pos[1] + 2) & 3)
    total = jnp.zeros((512, 512), F32)
    for group, part in zip(groups, (s0, s1, s2, s3)):
        total += jnp.dot(alpha[group], part[...], preferred_element_type=F32)
    out[...] = total.astype(F32).reshape(4, 128, 512)


def expect(pos, alpha, parts):
    return pl.pallas_call(
        expect_kernel,
        in_specs=[SM] + [VM] * 5,
        out_specs=VM,
        out_shape=jax.ShapeDtypeStruct((4, 128, 512), F32),
        compiler_params=params(32),
        name="expect",
    )(pos, alpha, *parts)


def count_kernel(transition, expected, counts, total):
    sums = jnp.zeros((128, 128), F32)
    for x in range(4):
        part = transition[:, x * 512 : (x + 1) * 512].astype(F32) * expected[x].astype(F32)
        counts[:, x * 512 : (x + 1) * 512] = part
        for i in range(4):
            sums += part[:, i * 128 : (i + 1) * 128]
    total[...] = jnp.sum(sums.T, axis=0, keepdims=True)


def count(transition, expected):
    return pl.pallas_call(
        count_kernel,
        in_specs=[VM] * 2,
        out_specs=[VM] * 2,
        out_shape=[jax.ShapeDtypeStruct((128, 2048), F32), jax.ShapeDtypeStruct((1, 128), F32)],
        compiler_params=params(32),
        name="count",
    )(transition, expected)


def divide_kernel(counts, totals, out):
    total = jnp.sum(totals[...].reshape(16, 128), axis=0, keepdims=True)
    column = jnp.broadcast_to(total, (128, 128)).T[:, :1]
    out[...] = (STATES * counts[...] / column).astype(BF16)


def divide(counts, totals):
    return pl.pallas_call(
        divide_kernel,
        in_specs=[VM] * 2,
        out_specs=VM,
        out_shape=jax.ShapeDtypeStruct((128, 2048), BF16),
        compiler_params=params(32),
        name="divide",
    )(counts, totals)


def ring(step, size=4):
    return [(i, (i + step) % size) for i in range(size)]


def per_device(ids, alpha, beta, emission, transition):
    y, x, z, k = (lax.axis_index(a) for a in ("y", "x", "z", "k"))
    pos = jnp.stack([y * 4 + x, y, x, k]).astype(jnp.int32)
    ids = ids.reshape(16, 128)

    alpha_all = lax.all_to_all(jnp.broadcast_to(alpha[None], (16, 128, 128)), ("z", "k"), 0, 0).reshape(2048, 128)
    alpha_all = lax.all_to_all(jnp.broadcast_to(alpha_all[None], (4, 2048, 128)), "x", 0, 0)
    alpha_t = turn(alpha_all)

    betas = []
    for d in range(4):
        piece = lax.dynamic_slice(beta, (0, ((x + d) & 3) * 512), (128, 512))
        betas.append(piece if d == 0 else lax.ppermute(piece, "x", ring(d)))

    picked = pick(pos, ids, emission).reshape(16, 32, 512)
    rows = lax.all_to_all(picked, ("y", "x"), 0, 0)
    own = scale(pos, ids, rows, betas).reshape(512, 512)

    ahead = [(a * 2 + c, ((a + (1 - 2 * c)) % 4) * 2 + c) for a in range(4) for c in range(2)]
    behind = [(b, a) for a, b in ahead]
    one = lax.ppermute(own, ("y", "k"), ahead)
    two = lax.ppermute(own, ("y", "k"), behind)
    far = lax.ppermute(one, ("y", "k"), ahead)

    expected = expect(pos, alpha_t, (own, one, two, far))
    expected = lax.all_to_all(expected, "x", 0, 0)
    counts, total = count(transition, expected)
    totals = lax.all_to_all(jnp.broadcast_to(total[None], (16, 1, 128)), ("z", "k"), 0, 0)
    return counts, divide(counts, totals)


def solution(mesh):
    fine = Mesh(np.asarray(mesh.devices).reshape(4, 4, 8, 2), ("y", "x", "z", "k"))
    row, col = ("y", "x"), ("z", "k")
    in_specs = (P(), P(col, row), P(row, col), P(row, col), P(row, col))
    out_specs = (P(row, col), P(row, col))
    return jax.shard_map(per_device, mesh=fine, in_specs=in_specs, out_specs=out_specs, check_vma=False)
```

```python
import jax
import jax.numpy as jnp
import numpy as np
from jax import lax
from jax.experimental import pallas as pl
from jax.experimental.pallas import tpu as pltpu
from jax.sharding import Mesh, PartitionSpec as P

STATES = 32768
RANGE = 2000
F32, BF16 = jnp.float32, jnp.bfloat16
VM = pl.BlockSpec(memory_space=pltpu.VMEM)
SM = pl.BlockSpec(memory_space=pltpu.SMEM)


SMALL = pl.CostEstimate(flops=1, bytes_accessed=1, transcendentals=0)


def iota(shape, dim):
    return lax.broadcasted_iota(jnp.int32, shape, dim)


def params(mib):
    return pltpu.CompilerParams(vmem_limit_bytes=mib << 20)


def cut_kernel(pos, a, o0, o1, o2, o3):
    for d, o in enumerate((o0, o1, o2, o3)):
        o[...] = a[:, pl.ds(pl.multiple_of(((pos[2] + d) & 3) * 512, 512), 512)]


def cut(pos, a):
    return pl.pallas_call(
        cut_kernel,
        in_specs=[SM, VM],
        out_specs=[VM] * 4,
        out_shape=[jax.ShapeDtypeStruct((128, 512), BF16)] * 4,
        compiler_params=params(8),
        cost_estimate=SMALL,
        name="cut",
    )(pos, a)


def pick_kernel(pos, ids, table, out, slab, sems):
    parts = ((0, 512), (512, 512), (1024, 512), (1536, 464))
    copies = [
        pltpu.make_async_copy(table.at[pl.ds(start, size)], slab.at[pl.ds(start, size)], sems.at[n])
        for n, (start, size) in enumerate(parts)
    ]
    for copy in copies:
        copy.start()
    local = ids[...] - pos[0] * RANGE
    mine = (local >= 0) & (local < RANGE)
    upto = (iota((128, 128), 0) <= iota((128, 128), 1)).astype(BF16)
    count = jnp.dot(mine.astype(F32).astype(BF16), upto, preferred_element_type=F32)
    value = jnp.where(mine, local, 0).astype(F32)
    count = jnp.where(mine, count, 0.0)
    wide = lambda a: jnp.broadcast_to(a[:, None, :], (16, 8, 128)).reshape(128, 128)
    order = ((iota((128, 128), 0) & 7) + 1).astype(F32)
    word = jnp.sum(jnp.where(wide(count) == order, wide(value), 0.0), axis=1, keepdims=True).astype(jnp.int32)
    rows = jnp.zeros((128, 2048), F32)
    for copy, (start, size) in zip(copies, parts):
        hot = (iota((128, size), 1) + start == word).astype(F32).astype(BF16)
        copy.wait()
        rows += jnp.dot(hot, slab[start : start + size, :], preferred_element_type=F32)
    for x in range(4):
        out[:, x] = rows[:, x * 512 : (x + 1) * 512].astype(BF16).reshape(4, 32, 512)


def pick(pos, ids, emission):
    return pl.pallas_call(
        pick_kernel,
        in_specs=[SM, VM, pl.BlockSpec(memory_space=pl.ANY)],
        out_specs=VM,
        out_shape=jax.ShapeDtypeStruct((4, 4, 32, 512), BF16),
        scratch_shapes=[pltpu.VMEM((RANGE, 2048), BF16), pltpu.SemaphoreType.DMA((4,))],
        compiler_params=params(58),
        cost_estimate=SMALL,
        name="pick",
    )(pos, ids, emission)


def scale_kernel(pos, ids, rows, c0, c1, c2, c3, out, wide):
    wide[...] = rows[...].astype(F32)
    before = (iota((128, 128), 0) < iota((128, 128), 1)).astype(BF16)
    for d, c in enumerate((c0, c1, c2, c3)):
        block = (pos[2] - d + 4) & 3
        word = ids[pl.ds(pos[1] * 4 + block, 1), :]
        wordb = jnp.broadcast_to(word, (16, 128))
        owner_at = iota((16, 128), 0)
        owns = (wordb >= owner_at * RANGE) & (wordb < (owner_at + 1) * RANGE)
        ownf = owns.astype(F32)
        earlier = jnp.dot(ownf.astype(BF16), before, preferred_element_type=F32)
        place = ownf * (earlier + (owner_at * 8).astype(F32))
        slot = jnp.sum(place, axis=0, keepdims=True).astype(jnp.int32)
        move = (iota((128, 128), 0) == slot).astype(F32).astype(BF16)
        given = wide[:, pl.ds(pl.multiple_of(block * 8, 8), 8), :].reshape(128, 512).astype(BF16)
        emitted = lax.dot_general(move, given, (((0,), (0,)), ((), ())), preferred_element_type=F32)
        out[block] = (emitted * c[...].astype(F32)).astype(BF16)


def scale(pos, ids, rows, cuts):
    return pl.pallas_call(
        scale_kernel,
        in_specs=[SM] + [VM] * 6,
        out_specs=VM,
        out_shape=jax.ShapeDtypeStruct((4, 128, 512), BF16),
        scratch_shapes=[pltpu.VMEM((16, 32, 512), F32)],
        compiler_params=params(16),
        cost_estimate=SMALL,
        name="scale",
    )(pos, ids, rows, *cuts)


def quarter(pos, transition, away):
    return transition[:, pl.ds(pl.multiple_of(((pos[2] + away + 4) & 3) * 512, 512), 512)]


def pack_kernel(pos, l0, l1, l2, l3, transition, ahead, behind):
    step = 1 - 2 * pos[3]
    near, far, back = (quarter(pos, transition, away) for away in (step, 2, -step))
    for n in range(4):
        lanes = slice(n * 128, (n + 1) * 128)
        ahead[n] = near[:, lanes]
        ahead[12 + n] = far[:, lanes]
        behind[n] = back[:, lanes]
    m = 0
    for part in (l0, l1, l2, l3):
        for n in range(part.shape[0]):
            ahead[4 + m] = part[n]
            behind[4 + m] = part[n]
            m += 1


def pack(pos, line, transition):
    return pl.pallas_call(
        pack_kernel,
        in_specs=[SM] + [VM] * 5,
        out_specs=[VM] * 2,
        out_shape=[jax.ShapeDtypeStruct((16, 128, 128), BF16), jax.ShapeDtypeStruct((12, 128, 128), BF16)],
        compiler_params=params(8),
        cost_estimate=SMALL,
        name="pack",
    )(pos, *line, transition)


def turn_kernel(pos, *refs):
    out = refs[8]
    for c in range(2):
        core = pos[3] ^ c
        step = 1 - 2 * core
        for n, (away, first) in enumerate(((0, 4), (-step, 4), (step, 4), (2, 0))):
            x = (pos[2] + away + 4) & 3
            for m, flip in enumerate((0, 1, 2, 3, 7, 6, 5, 4)):
                block = (pos[4] ^ flip) * 2 + core
                rows = pl.ds(pl.multiple_of(x * 128, 128), 128)
                times = pl.ds(pl.multiple_of((block & 3) * 128, 128), 128)
                out[block >> 2, rows, times] = refs[c * 4 + n][first + m].T


def turn(pos, parts):
    return pl.pallas_call(
        turn_kernel,
        in_specs=[SM] + [VM] * 8,
        out_specs=VM,
        out_shape=jax.ShapeDtypeStruct((4, 512, 512), BF16),
        compiler_params=params(16),
        cost_estimate=SMALL,
        name="turn",
    )(pos, *parts)


def expect_kernel(pos, alpha, s0, s1, s2, s3, transition, t1, t2, t3, total, sums):
    step = 1 - 2 * pos[3]
    groups = (pos[1], (pos[1] - step + 4) & 3, (pos[1] + step + 4) & 3, (pos[1] + 2) & 3)
    acc = jnp.zeros((512, 512), F32)
    for group, part in zip(groups, (s0, s1, s2, s3)):
        acc += jnp.dot(alpha[group], part[...], preferred_element_type=F32)
    total[...] = acc.reshape(4, 128, 512)
    for t, first, away in ((None, 0, 0), (t1, 0, -step), (t2, 0, step), (t3, 8, 2)):
        block = (pos[2] + away + 4) & 3
        lanes = jnp.zeros((128, 128), F32)
        if t is None:
            mine = quarter(pos, transition, 0)
        for n in range(4):
            part = slice(n * 128, (n + 1) * 128)
            weight = mine[:, part] if t is None else t[first + n]
            lanes += weight.astype(F32) * total[block, :, part]
        line = jnp.sum(lanes.T, axis=0, keepdims=True)
        sums[pl.ds(block * 16, 16)] = jnp.broadcast_to(line[None], (16, 1, 128))


def expect(pos, alpha, parts, transition, quarters):
    return pl.pallas_call(
        expect_kernel,
        in_specs=[SM] + [VM] * 9,
        out_specs=[VM] * 2,
        out_shape=[jax.ShapeDtypeStruct((4, 128, 512), F32), jax.ShapeDtypeStruct((64, 1, 128), F32)],
        compiler_params=params(24),
        cost_estimate=SMALL,
        name="expect",
    )(pos, alpha, *parts, transition, *quarters)


def code_kernel(pos, total, *outs):
    for d, out in enumerate(outs, 1):
        power = total[(pos[2] + d) & 3]
        power = power * power
        power = power * power
        out[...] = (power * power).astype(BF16)


def code(pos, total):
    return pl.pallas_call(
        code_kernel,
        in_specs=[SM, VM],
        out_specs=[VM] * 3,
        out_shape=[jax.ShapeDtypeStruct((128, 512), BF16)] * 3,
        compiler_params=params(8),
        cost_estimate=pl.CostEstimate(flops=10**9, bytes_accessed=10**7, transcendentals=0),
        name="code",
    )(pos, total)


def column_kernel(sums, out):
    whole = jnp.sum(sums[...].reshape(64, 128), axis=0, keepdims=True)
    out[...] = STATES / jnp.broadcast_to(whole, (128, 128)).T


def column(sums):
    return pl.pallas_call(
        column_kernel,
        in_specs=[VM],
        out_specs=VM,
        out_shape=jax.ShapeDtypeStruct((128, 128), F32),
        compiler_params=params(8),
        cost_estimate=pl.CostEstimate(flops=int(2 * 10**9), bytes_accessed=10**6, transcendentals=0),
        name="column",
    )(sums)


def finish_kernel(pos, transition, total, e1, e2, e3, rate, counts, out):
    for d, e in enumerate((None, e1, e2, e3)):
        part = pl.ds(pl.multiple_of(((pos[2] - d + 4) & 3) * 512, 512), 512)
        if d:
            expected = jnp.sqrt(jnp.sqrt(jnp.sqrt(e[...].astype(F32))))
        else:
            expected = total[pos[2]]
        count = transition[:, part].astype(F32) * expected
        counts[:, part] = count
        out[:, part] = (count * jnp.concatenate([rate[...]] * 4, axis=1)).astype(BF16)


def finish(pos, transition, total, parts, rate):
    return pl.pallas_call(
        finish_kernel,
        in_specs=[SM] + [VM] * 6,
        out_specs=[VM] * 2,
        out_shape=[jax.ShapeDtypeStruct((128, 2048), F32), jax.ShapeDtypeStruct((128, 2048), BF16)],
        compiler_params=params(16),
        cost_estimate=SMALL,
        name="finish",
    )(pos, transition, total, *parts, rate)


def ring(step, size=4):
    return [(i, (i + step) % size) for i in range(size)]


def per_device(ids, alpha, beta, emission, transition):
    y, x, z, k = (lax.axis_index(a) for a in ("y", "x", "z", "k"))
    pos = jnp.stack([y * 4 + x, y, x, k, z]).astype(jnp.int32)
    ids = ids.reshape(16, 128)
    ahead = [(a * 2 + c, ((a + 1 - 2 * c) % 4) * 2 + c) for a in range(4) for c in range(2)]
    behind = [(b, a) for a, b in ahead]
    swap = [(0, 1), (1, 0)]

    together = lax.optimization_barrier
    flip = lambda a, by: lax.ppermute(a, "z", [(i, i ^ by) for i in range(8)])

    line = [alpha[None], flip(alpha[None], 1)]
    betas = [c if d == 0 else lax.ppermute(c, "x", ring(d)) for d, c in enumerate(cut(pos, beta))]
    picked = pick(pos, ids, emission)
    picked, line, betas = together((picked, line, betas))

    rows = lax.all_to_all(picked.reshape(16, 32, 512), ("y", "x"), 0, 0)
    line.append(flip(jnp.concatenate(line), 2))
    line.append(flip(jnp.concatenate(line), 7))
    rows, line = together((rows, line))
    own = scale(pos, ids, rows, betas).reshape(512, 512)

    own, line = together((own, line))
    one = lax.ppermute(own, ("y", "k"), ahead)
    two = lax.ppermute(own, ("y", "k"), behind)
    to_a, to_b = pack(pos, line, transition)
    one_a = lax.ppermute(to_a, ("x", "k"), ahead)
    two_a = lax.ppermute(to_b, ("x", "k"), behind)

    one, two, one_a, two_a, to_b = together((one, two, one_a, two_a, to_b))
    far = lax.ppermute(one, ("y", "k"), ahead)
    far_a = lax.ppermute(one_a[4:], ("x", "k"), ahead)
    sources = [to_b, one_a, two_a, far_a]
    sources += [lax.ppermute(a, "k", swap) for a in sources]
    alpha_t = turn(pos, sources)

    total, sums = expect(pos, alpha_t, (own, one, two, far), transition, (one_a, two_a, far_a))
    sums = lax.all_to_all(sums, ("x", "z", "k"), 0, 0)
    parts = [lax.ppermute(e, "x", ring(d)) for d, e in enumerate(code(pos, total), 1)]
    return finish(pos, transition, total, parts, column(sums))


def solution(mesh):
    fine = Mesh(np.asarray(mesh.devices).reshape(4, 4, 8, 2), ("y", "x", "z", "k"))
    row, col = ("y", "x"), ("z", "k")
    in_specs = (P(), P(col, row), P(row, col), P(row, col), P(row, col))
    out_specs = (P(row, col), P(row, col))
    return jax.shard_map(per_device, mesh=fine, in_specs=in_specs, out_specs=out_specs, check_vma=False)
```

```python
import jax
import jax.numpy as jnp
import numpy as np
from jax import lax
from jax.experimental import pallas as pl
from jax.experimental.pallas import tpu as pltpu
from jax.sharding import Mesh, PartitionSpec as P

STATES = 32768
RANGE = 2000
F32, BF16 = jnp.float32, jnp.bfloat16
VM = pl.BlockSpec(memory_space=pltpu.VMEM)
SM = pl.BlockSpec(memory_space=pltpu.SMEM)


SMALL = pl.CostEstimate(flops=1, bytes_accessed=1, transcendentals=0)


def iota(shape, dim):
    return lax.broadcasted_iota(jnp.int32, shape, dim)


def params(mib):
    return pltpu.CompilerParams(vmem_limit_bytes=mib << 20)


def cut_kernel(pos, a, o0, o1, o2, o3):
    for d, o in enumerate((o0, o1, o2, o3)):
        o[...] = a[:, pl.ds(pl.multiple_of(((pos[2] + d) & 3) * 512, 512), 512)]


def cut(pos, a):
    return pl.pallas_call(
        cut_kernel,
        in_specs=[SM, VM],
        out_specs=[VM] * 4,
        out_shape=[jax.ShapeDtypeStruct((128, 512), BF16)] * 4,
        compiler_params=params(8),
        cost_estimate=SMALL,
        name="cut",
    )(pos, a)


def pick_kernel(pos, ids, table, out, slab, sems):
    parts = ((0, 512), (512, 512), (1024, 512), (1536, 464))
    copies = [
        pltpu.make_async_copy(table.at[pl.ds(start, size)], slab.at[pl.ds(start, size)], sems.at[n])
        for n, (start, size) in enumerate(parts)
    ]
    for copy in copies:
        copy.start()
    local = ids[...] - pos[0] * RANGE
    mine = (local >= 0) & (local < RANGE)
    upto = (iota((128, 128), 0) <= iota((128, 128), 1)).astype(BF16)
    count = jnp.dot(mine.astype(F32).astype(BF16), upto, preferred_element_type=F32)
    value = jnp.where(mine, local, 0).astype(F32)
    count = jnp.where(mine, count, 0.0)
    wide = lambda a: jnp.broadcast_to(a[:, None, :], (16, 8, 128)).reshape(128, 128)
    order = ((iota((128, 128), 0) & 7) + 1).astype(F32)
    word = jnp.sum(jnp.where(wide(count) == order, wide(value), 0.0), axis=1, keepdims=True).astype(jnp.int32)
    rows = jnp.zeros((128, 2048), F32)
    for copy, (start, size) in zip(copies, parts):
        hot = (iota((128, size), 1) + start == word).astype(F32).astype(BF16)
        copy.wait()
        rows += jnp.dot(hot, slab[start : start + size, :], preferred_element_type=F32)
    for x in range(4):
        out[:, x] = rows[:, x * 512 : (x + 1) * 512].astype(BF16).reshape(4, 32, 512)


def pick(pos, ids, emission):
    return pl.pallas_call(
        pick_kernel,
        in_specs=[SM, VM, pl.BlockSpec(memory_space=pl.ANY)],
        out_specs=VM,
        out_shape=jax.ShapeDtypeStruct((4, 4, 32, 512), BF16),
        scratch_shapes=[pltpu.VMEM((RANGE, 2048), BF16), pltpu.SemaphoreType.DMA((4,))],
        compiler_params=params(58),
        cost_estimate=SMALL,
        name="pick",
    )(pos, ids, emission)


def scale_kernel(pos, ids, rows, c0, c1, c2, c3, out, wide):
    wide[...] = rows[...].astype(F32)
    before = (iota((128, 128), 0) < iota((128, 128), 1)).astype(BF16)
    for d, c in enumerate((c0, c1, c2, c3)):
        block = (pos[2] - d + 4) & 3
        word = ids[pl.ds(pos[1] * 4 + block, 1), :]
        wordb = jnp.broadcast_to(word, (16, 128))
        owner_at = iota((16, 128), 0)
        owns = (wordb >= owner_at * RANGE) & (wordb < (owner_at + 1) * RANGE)
        ownf = owns.astype(F32)
        earlier = jnp.dot(ownf.astype(BF16), before, preferred_element_type=F32)
        place = ownf * (earlier + (owner_at * 8).astype(F32))
        slot = jnp.sum(place, axis=0, keepdims=True).astype(jnp.int32)
        move = (iota((128, 128), 0) == slot).astype(F32).astype(BF16)
        given = wide[:, pl.ds(pl.multiple_of(block * 8, 8), 8), :].reshape(128, 512).astype(BF16)
        emitted = lax.dot_general(move, given, (((0,), (0,)), ((), ())), preferred_element_type=F32)
        out[block] = (emitted * c[...].astype(F32)).astype(BF16)


def scale(pos, ids, rows, cuts):
    return pl.pallas_call(
        scale_kernel,
        in_specs=[SM] + [VM] * 6,
        out_specs=VM,
        out_shape=jax.ShapeDtypeStruct((4, 128, 512), BF16),
        scratch_shapes=[pltpu.VMEM((16, 32, 512), F32)],
        compiler_params=params(16),
        cost_estimate=pl.CostEstimate(flops=10**10, bytes_accessed=10**7, transcendentals=0),
        name="scale",
    )(pos, ids, rows, *cuts)


def quarter(pos, transition, away):
    return transition[:, pl.ds(pl.multiple_of(((pos[2] + away + 4) & 3) * 512, 512), 512)]


def join_kernel(l0, l1, l2, out):
    out[0:1] = l0[...]
    out[1:2] = l1[...]
    out[2:4] = l2[...]


def join(line):
    return pl.pallas_call(
        join_kernel,
        in_specs=[VM] * 3,
        out_specs=VM,
        out_shape=jax.ShapeDtypeStruct((4, 128, 128), BF16),
        compiler_params=params(8),
        cost_estimate=pl.CostEstimate(flops=3 * 10**10, bytes_accessed=10**6, transcendentals=0),
        name="join",
    )(*line)


def pack_kernel(pos, l0, l1, l2, l3, transition, ahead, behind):
    step = 1 - 2 * pos[3]
    near, far, back = (quarter(pos, transition, away) for away in (step, 2, -step))
    for n in range(4):
        lanes = slice(n * 128, (n + 1) * 128)
        ahead[n] = near[:, lanes]
        ahead[12 + n] = far[:, lanes]
        behind[n] = back[:, lanes]
    m = 0
    for part in (l0, l1, l2, l3):
        for n in range(part.shape[0]):
            ahead[4 + m] = part[n]
            behind[4 + m] = part[n]
            m += 1


def pack(pos, line, transition):
    return pl.pallas_call(
        pack_kernel,
        in_specs=[SM] + [VM] * 5,
        out_specs=[VM] * 2,
        out_shape=[jax.ShapeDtypeStruct((16, 128, 128), BF16), jax.ShapeDtypeStruct((12, 128, 128), BF16)],
        compiler_params=params(8),
        cost_estimate=SMALL,
        name="pack",
    )(pos, *line, transition)


def turn_kernel(pos, *refs):
    out = refs[8]
    for c in range(2):
        core = pos[3] ^ c
        step = 1 - 2 * core
        for n, (away, first) in enumerate(((0, 4), (-step, 4), (step, 4), (2, 0))):
            x = (pos[2] + away + 4) & 3
            for m, flip in enumerate((0, 1, 2, 3, 7, 6, 5, 4)):
                block = (pos[4] ^ flip) * 2 + core
                rows = pl.ds(pl.multiple_of(x * 128, 128), 128)
                times = pl.ds(pl.multiple_of((block & 3) * 128, 128), 128)
                out[block >> 2, rows, times] = refs[c * 4 + n][first + m].T


def turn(pos, parts):
    return pl.pallas_call(
        turn_kernel,
        in_specs=[SM] + [VM] * 8,
        out_specs=VM,
        out_shape=jax.ShapeDtypeStruct((4, 512, 512), BF16),
        compiler_params=params(16),
        cost_estimate=SMALL,
        name="turn",
    )(pos, *parts)


def expect_kernel(pos, alpha, s0, s1, s2, s3, transition, t1, t2, t3, total, sums, e1, e2, e3):
    step = 1 - 2 * pos[3]
    groups = (pos[1], (pos[1] - step + 4) & 3, (pos[1] + step + 4) & 3, (pos[1] + 2) & 3)
    acc = jnp.zeros((512, 512), F32)
    for group, part in zip(groups, (s0, s1, s2, s3)):
        acc += jnp.dot(alpha[group], part[...], preferred_element_type=F32)
    total[...] = acc.reshape(4, 128, 512)
    for d, e in enumerate((e1, e2, e3), 1):
        power = total[(pos[2] + d) & 3]
        power = power * power
        power = power * power
        e[...] = (power * power).astype(BF16)
    for t, first, away in ((None, 0, 0), (t1, 0, -step), (t2, 0, step), (t3, 8, 2)):
        block = (pos[2] + away + 4) & 3
        lanes = jnp.zeros((128, 128), F32)
        if t is None:
            mine = quarter(pos, transition, 0)
        for n in range(4):
            part = slice(n * 128, (n + 1) * 128)
            weight = mine[:, part] if t is None else t[first + n]
            lanes += weight.astype(F32) * total[block, :, part]
        line = jnp.sum(lanes.T, axis=0, keepdims=True)
        sums[pl.ds(block, 1)] = line[None]


def expect(pos, alpha, parts, transition, quarters):
    return pl.pallas_call(
        expect_kernel,
        in_specs=[SM] + [VM] * 9,
        out_specs=[VM] * 5,
        out_shape=[
            jax.ShapeDtypeStruct((4, 128, 512), F32),
            jax.ShapeDtypeStruct((4, 1, 128), F32),
            *[jax.ShapeDtypeStruct((128, 512), BF16)] * 3,
        ],
        compiler_params=params(24),
        cost_estimate=SMALL,
        name="expect",
    )(pos, alpha, *parts, transition, *quarters)


def column_kernel(sums, out):
    whole = jnp.sum(sums[...].reshape(32, 128), axis=0, keepdims=True)
    out[...] = STATES / jnp.broadcast_to(whole, (128, 128)).T


def column(sums):
    return pl.pallas_call(
        column_kernel,
        in_specs=[VM],
        out_specs=VM,
        out_shape=jax.ShapeDtypeStruct((128, 128), F32),
        compiler_params=params(8),
        cost_estimate=pl.CostEstimate(flops=int(2 * 10**9), bytes_accessed=10**6, transcendentals=0),
        name="column",
    )(sums)


def finish_kernel(pos, transition, total, e1, e2, e3, rate, counts, out, kept, rounded, sems):
    copies = []
    for d, e in enumerate((None, e1, e2, e3)):
        part = pl.ds(pl.multiple_of(((pos[2] - d + 4) & 3) * 512, 512), 512)
        if d:
            root = lax.rsqrt(lax.rsqrt(e[...].astype(F32)))
            expected = root * lax.rsqrt(root)
        else:
            expected = total[pos[2]]
        count = transition[:, part].astype(F32) * expected
        kept[d] = count
        rounded[d] = (count * jnp.concatenate([rate[...]] * 4, axis=1)).astype(BF16)
        copies.append(pltpu.make_async_copy(kept.at[d], counts.at[:, part], sems.at[2 * d]))
        copies.append(pltpu.make_async_copy(rounded.at[d], out.at[:, part], sems.at[2 * d + 1]))
        copies[-2].start()
        copies[-1].start()
    for copy in copies:
        copy.wait()


def finish(pos, transition, total, parts, rate):
    return pl.pallas_call(
        finish_kernel,
        in_specs=[SM] + [VM] * 6,
        out_specs=[pl.BlockSpec(memory_space=pl.ANY)] * 2,
        out_shape=[jax.ShapeDtypeStruct((128, 2048), F32), jax.ShapeDtypeStruct((128, 2048), BF16)],
        scratch_shapes=[
            pltpu.VMEM((4, 128, 512), F32),
            pltpu.VMEM((4, 128, 512), BF16),
            pltpu.SemaphoreType.DMA((8,)),
        ],
        compiler_params=params(16),
        cost_estimate=SMALL,
        name="finish",
    )(pos, transition, total, *parts, rate)


def ring(step, size=4):
    return [(i, (i + step) % size) for i in range(size)]


def per_device(ids, alpha, beta, emission, transition):
    y, x, z, k = (lax.axis_index(a) for a in ("y", "x", "z", "k"))
    pos = jnp.stack([y * 4 + x, y, x, k, z]).astype(jnp.int32)
    ids = ids.reshape(16, 128)
    ahead = [(a * 2 + c, ((a + 1 - 2 * c) % 4) * 2 + c) for a in range(4) for c in range(2)]
    behind = [(b, a) for a, b in ahead]
    swap = [(0, 1), (1, 0)]

    together = lax.optimization_barrier
    flip = lambda a, by: lax.ppermute(a, "z", [(i, i ^ by) for i in range(8)])

    line = [alpha[None], flip(alpha[None], 1)]
    betas = [c if d == 0 else lax.ppermute(c, "x", ring(d)) for d, c in enumerate(cut(pos, beta))]
    picked = pick(pos, ids, emission)
    picked, line, betas = together((picked, line, betas))

    rows = lax.all_to_all(picked.reshape(16, 32, 512), ("y", "x"), 0, 0)
    line.append(flip(jnp.concatenate(line), 2))
    line.append(flip(join(line), 7))
    own = scale(pos, ids, rows, betas).reshape(512, 512)

    one = lax.ppermute(own, ("y", "k"), ahead)
    two = lax.ppermute(own, ("y", "k"), behind)
    to_a, to_b = pack(pos, line, transition)
    one_a = lax.ppermute(to_a, ("x", "k"), ahead)
    two_a = lax.ppermute(to_b, ("x", "k"), behind)

    far = lax.ppermute(one, ("y", "k"), ahead)
    far_a = lax.ppermute(one_a[4:], ("x", "k"), ahead)
    far_a, two = together((far_a, two))
    sources = [to_b, one_a, two_a, far_a]
    sources += [lax.ppermute(a, "k", swap) for a in sources]
    alpha_t = turn(pos, sources)

    total, sums, *parts = expect(pos, alpha_t, (own, one, two, far), transition, (one_a, two_a, far_a))
    sums = sums + lax.ppermute(sums, "k", swap)
    sums = jnp.broadcast_to(sums[:, None], (4, 8, 1, 128)).reshape(32, 1, 128)
    sums = lax.all_to_all(sums, ("x", "z"), 0, 0)
    parts = [lax.ppermute(e, "x", ring(d)) for d, e in enumerate(parts, 1)]
    return finish(pos, transition, total, parts, column(sums))


def solution(mesh):
    fine = Mesh(np.asarray(mesh.devices).reshape(4, 4, 8, 2), ("y", "x", "z", "k"))
    row, col = ("y", "x"), ("z", "k")
    in_specs = (P(), P(col, row), P(row, col), P(row, col), P(row, col))
    out_specs = (P(row, col), P(row, col))
    return jax.shard_map(per_device, mesh=fine, in_specs=in_specs, out_specs=out_specs, check_vma=False)
```

```python
import jax
import jax.numpy as jnp
import numpy as np
from jax import lax
from jax.experimental import pallas as pl
from jax.experimental.pallas import tpu as pltpu
from jax.sharding import Mesh, PartitionSpec as P

STATES = 32768
RANGE = 2000
F32, BF16 = jnp.float32, jnp.bfloat16
VM = pl.BlockSpec(memory_space=pltpu.VMEM)
SM = pl.BlockSpec(memory_space=pltpu.SMEM)


SMALL = pl.CostEstimate(flops=1, bytes_accessed=1, transcendentals=0)


def iota(shape, dim):
    return lax.broadcasted_iota(jnp.int32, shape, dim)


def params(mib):
    return pltpu.CompilerParams(vmem_limit_bytes=mib << 20)


def cut_kernel(pos, a, o0, o1, o2, o3):
    for d, o in enumerate((o0, o1, o2, o3)):
        o[...] = a[:, pl.ds(pl.multiple_of(((pos[2] + d) & 3) * 512, 512), 512)]


def cut(pos, a):
    return pl.pallas_call(
        cut_kernel,
        in_specs=[SM, VM],
        out_specs=[VM] * 4,
        out_shape=[jax.ShapeDtypeStruct((128, 512), BF16)] * 4,
        compiler_params=params(8),
        cost_estimate=SMALL,
        name="cut",
    )(pos, a)


def pick_kernel(pos, ids, table, out, slab, sems):
    parts = ((0, 512), (512, 512), (1024, 512), (1536, 464))
    copies = [
        pltpu.make_async_copy(table.at[pl.ds(start, size)], slab.at[pl.ds(start, size)], sems.at[n])
        for n, (start, size) in enumerate(parts)
    ]
    for copy in copies:
        copy.start()
    local = ids[...] - pos[0] * RANGE
    mine = (local >= 0) & (local < RANGE)
    upto = (iota((128, 128), 0) <= iota((128, 128), 1)).astype(BF16)
    count = jnp.dot(mine.astype(F32).astype(BF16), upto, preferred_element_type=F32)
    value = jnp.where(mine, local, 0).astype(F32)
    count = jnp.where(mine, count, 0.0)
    wide = lambda a: jnp.broadcast_to(a[:, None, :], (16, 8, 128)).reshape(128, 128)
    order = ((iota((128, 128), 0) & 7) + 1).astype(F32)
    word = jnp.sum(jnp.where(wide(count) == order, wide(value), 0.0), axis=1, keepdims=True).astype(jnp.int32)
    rows = jnp.zeros((128, 2048), F32)
    for copy, (start, size) in zip(copies, parts):
        hot = (iota((128, size), 1) + start == word).astype(F32).astype(BF16)
        copy.wait()
        rows += jnp.dot(hot, slab[start : start + size, :], preferred_element_type=F32)
    for x in range(4):
        out[:, x] = rows[:, x * 512 : (x + 1) * 512].astype(BF16).reshape(4, 32, 512)


def pick(pos, ids, emission):
    return pl.pallas_call(
        pick_kernel,
        in_specs=[SM, VM, pl.BlockSpec(memory_space=pl.ANY)],
        out_specs=VM,
        out_shape=jax.ShapeDtypeStruct((4, 4, 32, 512), BF16),
        scratch_shapes=[pltpu.VMEM((RANGE, 2048), BF16), pltpu.SemaphoreType.DMA((4,))],
        compiler_params=params(58),
        cost_estimate=SMALL,
        name="pick",
    )(pos, ids, emission)


def moves_kernel(pos, ids, out):
    before = (iota((128, 128), 0) < iota((128, 128), 1)).astype(BF16)
    for block in range(4):
        word = ids[pl.ds(pos[1] * 4 + block, 1), :]
        wordb = jnp.broadcast_to(word, (16, 128))
        owner_at = iota((16, 128), 0)
        owns = (wordb >= owner_at * RANGE) & (wordb < (owner_at + 1) * RANGE)
        ownf = owns.astype(F32)
        earlier = jnp.dot(ownf.astype(BF16), before, preferred_element_type=F32)
        place = ownf * (earlier + (owner_at * 8).astype(F32))
        slot = jnp.sum(place, axis=0, keepdims=True).astype(jnp.int32)
        out[block] = (iota((128, 128), 0) == slot).astype(F32).T.astype(BF16)


def moves(pos, ids):
    return pl.pallas_call(
        moves_kernel,
        in_specs=[SM, VM],
        out_specs=VM,
        out_shape=jax.ShapeDtypeStruct((4, 128, 128), BF16),
        compiler_params=params(8),
        cost_estimate=SMALL,
        name="moves",
    )(pos, ids)


def scale_kernel(pos, move, rows, c0, c1, c2, c3, out, wide):
    wide[...] = rows[...].astype(F32)
    for d, c in enumerate((c0, c1, c2, c3)):
        block = (pos[2] - d + 4) & 3
        given = wide[:, pl.ds(pl.multiple_of(block * 8, 8), 8), :].reshape(128, 512).astype(BF16)
        emitted = jnp.dot(move[block], given, preferred_element_type=F32)
        out[block] = (emitted * c[...].astype(F32)).astype(BF16)


def scale(pos, move, rows, cuts):
    return pl.pallas_call(
        scale_kernel,
        in_specs=[SM] + [VM] * 6,
        out_specs=VM,
        out_shape=jax.ShapeDtypeStruct((4, 128, 512), BF16),
        scratch_shapes=[pltpu.VMEM((16, 32, 512), F32)],
        compiler_params=params(16),
        cost_estimate=pl.CostEstimate(flops=10**10, bytes_accessed=10**7, transcendentals=0),
        name="scale",
    )(pos, move, rows, *cuts)


def quarter(pos, transition, away):
    return transition[:, pl.ds(pl.multiple_of(((pos[2] + away + 4) & 3) * 512, 512), 512)]


def join_kernel(l0, l1, l2, out):
    out[0:1] = l0[...]
    out[1:2] = l1[...]
    out[2:4] = l2[...]


def join(line):
    return pl.pallas_call(
        join_kernel,
        in_specs=[VM] * 3,
        out_specs=VM,
        out_shape=jax.ShapeDtypeStruct((4, 128, 128), BF16),
        compiler_params=params(8),
        cost_estimate=pl.CostEstimate(flops=3 * 10**10, bytes_accessed=10**6, transcendentals=0),
        name="join",
    )(*line)


def pack_kernel(pos, l0, l1, l2, l3, transition, ahead, behind):
    step = 1 - 2 * pos[3]
    near, far, back = (quarter(pos, transition, away) for away in (step, 2, -step))
    for n in range(4):
        lanes = slice(n * 128, (n + 1) * 128)
        ahead[n] = near[:, lanes]
        ahead[12 + n] = far[:, lanes]
        behind[n] = back[:, lanes]
    m = 0
    for part in (l0, l1, l2, l3):
        for n in range(part.shape[0]):
            ahead[4 + m] = part[n]
            behind[4 + m] = part[n]
            m += 1


def pack(pos, line, transition):
    return pl.pallas_call(
        pack_kernel,
        in_specs=[SM] + [VM] * 5,
        out_specs=[VM] * 2,
        out_shape=[jax.ShapeDtypeStruct((16, 128, 128), BF16), jax.ShapeDtypeStruct((12, 128, 128), BF16)],
        compiler_params=params(8),
        cost_estimate=SMALL,
        name="pack",
    )(pos, *line, transition)


def turn_kernel(pos, *refs):
    out = refs[8]
    for c in range(2):
        core = pos[3] ^ c
        step = 1 - 2 * core
        for n, (away, first) in enumerate(((0, 4), (-step, 4 - 4 * c), (step, 4), (2, 0))):
            x = (pos[2] + away + 4) & 3
            for m, flip in enumerate((0, 2, 6, 4, 1, 3, 7, 5)):
                block = (pos[4] ^ flip) * 2 + core
                rows = pl.ds(pl.multiple_of(x * 128, 128), 128)
                times = pl.ds(pl.multiple_of((block & 3) * 128, 128), 128)
                out[block >> 2, rows, times] = refs[c * 4 + n][first + m].T


def turn(pos, parts):
    return pl.pallas_call(
        turn_kernel,
        in_specs=[SM] + [VM] * 8,
        out_specs=VM,
        out_shape=jax.ShapeDtypeStruct((4, 512, 512), BF16),
        compiler_params=params(16),
        cost_estimate=SMALL,
        name="turn",
    )(pos, *parts)


def expect_kernel(pos, alpha, s0, s1, s2, s3, transition, t1, t2, t3, total, sums, e1, e2, e3):
    step = 1 - 2 * pos[3]
    groups = (pos[1], (pos[1] - step + 4) & 3, (pos[1] + step + 4) & 3, (pos[1] + 2) & 3)
    acc = jnp.zeros((512, 512), F32)
    for group, part in zip(groups, (s0, s1, s2, s3)):
        acc += jnp.dot(alpha[group], part[...], preferred_element_type=F32)
    total[...] = acc.reshape(4, 128, 512)
    for d, e in enumerate((e1, e2, e3), 1):
        power = total[(pos[2] + d) & 3]
        power = power * power
        power = power * power
        e[...] = (power * power).astype(BF16)
    for t, first, away in ((None, 0, 0), (t1, 0, -step), (t2, 0, step), (t3, 8, 2)):
        block = (pos[2] + away + 4) & 3
        lanes = jnp.zeros((128, 128), F32)
        if t is None:
            mine = quarter(pos, transition, 0)
        for n in range(4):
            part = slice(n * 128, (n + 1) * 128)
            weight = mine[:, part] if t is None else t[first + n]
            lanes += weight.astype(F32) * total[block, :, part]
        line = jnp.sum(lanes.T, axis=0, keepdims=True)
        sums[pl.ds(block, 1)] = line[None]


def expect(pos, alpha, parts, transition, quarters):
    return pl.pallas_call(
        expect_kernel,
        in_specs=[SM] + [VM] * 9,
        out_specs=[VM] * 5,
        out_shape=[
            jax.ShapeDtypeStruct((4, 128, 512), F32),
            jax.ShapeDtypeStruct((4, 1, 128), F32),
            *[jax.ShapeDtypeStruct((128, 512), BF16)] * 3,
        ],
        compiler_params=params(24),
        cost_estimate=SMALL,
        name="expect",
    )(pos, alpha, *parts, transition, *quarters)


def column_kernel(sums, out):
    whole = jnp.sum(sums[...].reshape(32, 128), axis=0, keepdims=True)
    out[...] = STATES / jnp.broadcast_to(whole, (128, 128)).T


def column(sums):
    return pl.pallas_call(
        column_kernel,
        in_specs=[VM],
        out_specs=VM,
        out_shape=jax.ShapeDtypeStruct((128, 128), F32),
        compiler_params=params(8),
        cost_estimate=pl.CostEstimate(flops=int(2 * 10**9), bytes_accessed=10**6, transcendentals=0),
        name="column",
    )(sums)


def finish_kernel(pos, transition, total, e1, e2, e3, rate, counts, out, kept, rounded, sems):
    copies = []
    for d, e in enumerate((None, e1, e2, e3)):
        part = pl.ds(pl.multiple_of(((pos[2] - d + 4) & 3) * 512, 512), 512)
        if d:
            root = lax.rsqrt(lax.rsqrt(e[...].astype(F32)))
            expected = root * lax.rsqrt(root)
        else:
            expected = total[pos[2]]
        count = transition[:, part].astype(F32) * expected
        kept[d] = count
        rounded[d] = (count * jnp.concatenate([rate[...]] * 4, axis=1)).astype(BF16)
        copies.append(pltpu.make_async_copy(kept.at[d], counts.at[:, part], sems.at[2 * d]))
        copies.append(pltpu.make_async_copy(rounded.at[d], out.at[:, part], sems.at[2 * d + 1]))
        copies[-2].start()
        copies[-1].start()
    for copy in copies:
        copy.wait()


def finish(pos, transition, total, parts, rate):
    return pl.pallas_call(
        finish_kernel,
        in_specs=[SM] + [VM] * 6,
        out_specs=[pl.BlockSpec(memory_space=pl.ANY)] * 2,
        out_shape=[jax.ShapeDtypeStruct((128, 2048), F32), jax.ShapeDtypeStruct((128, 2048), BF16)],
        scratch_shapes=[
            pltpu.VMEM((4, 128, 512), F32),
            pltpu.VMEM((4, 128, 512), BF16),
            pltpu.SemaphoreType.DMA((8,)),
        ],
        compiler_params=params(16),
        cost_estimate=SMALL,
        name="finish",
    )(pos, transition, total, *parts, rate)


def ring(step, size=4):
    return [(i, (i + step) % size) for i in range(size)]


def per_device(ids, alpha, beta, emission, transition):
    y, x, z, k = (lax.axis_index(a) for a in ("y", "x", "z", "k"))
    pos = jnp.stack([y * 4 + x, y, x, k, z]).astype(jnp.int32)
    ids = ids.reshape(16, 128)
    ahead = [(a * 2 + c, ((a + 1 - 2 * c) % 4) * 2 + c) for a in range(4) for c in range(2)]
    behind = [(b, a) for a, b in ahead]
    swap = [(0, 1), (1, 0)]

    together = lax.optimization_barrier
    flip = lambda a, by: lax.ppermute(a, "z", [(i, i ^ by) for i in range(8)])

    line = [alpha[None], flip(alpha[None], 2)]
    betas = [c if d == 0 else lax.ppermute(c, "x", ring(d)) for d, c in enumerate(cut(pos, beta))]
    picked = pick(pos, ids, emission)
    picked, line, betas = together((picked, line, betas))

    rows = lax.all_to_all(picked.reshape(16, 32, 512), ("y", "x"), 0, 0)
    line.append(flip(jnp.concatenate(line), 6))
    line.append(flip(join(line), 1))
    ids, _ = together((ids, line[2]))
    own = scale(pos, moves(pos, ids), rows, betas).reshape(512, 512)

    one = lax.ppermute(own, ("y", "k"), ahead)
    two = lax.ppermute(own, ("y", "k"), behind)
    to_a, to_b = pack(pos, line, transition)
    one_a = lax.ppermute(to_a, ("x", "k"), ahead)
    later, one_a = together((to_b, one_a))
    two_a = lax.ppermute(later, ("x", "k"), behind)

    far = lax.ppermute(one, ("y", "k"), ahead)
    one_c = one_a[4:]
    far_a = lax.ppermute(one_c, ("x", "k"), ahead)
    one_c, far_a, two = together((one_c, far_a, two))
    sources = [to_b, one_a, two_a, far_a]
    sources += [lax.ppermute(a, "k", swap) for a in (to_b, one_c, two_a, far_a)]
    alpha_t = turn(pos, sources)

    total, sums, *parts = expect(pos, alpha_t, (own, one, two, far), transition, (one_a, two_a, far_a))
    sums = sums + lax.ppermute(sums, "k", swap)
    sums = jnp.broadcast_to(sums[:, None], (4, 8, 1, 128)).reshape(32, 1, 128)
    sums = lax.all_to_all(sums, ("x", "z"), 0, 0)
    parts = [lax.ppermute(e, "x", ring(d)) for d, e in enumerate(parts, 1)]
    return finish(pos, transition, total, parts, column(sums))


def solution(mesh):
    fine = Mesh(np.asarray(mesh.devices).reshape(4, 4, 8, 2), ("y", "x", "z", "k"))
    row, col = ("y", "x"), ("z", "k")
    in_specs = (P(), P(col, row), P(row, col), P(row, col), P(row, col))
    out_specs = (P(row, col), P(row, col))
    return jax.shard_map(per_device, mesh=fine, in_specs=in_specs, out_specs=out_specs, check_vma=False)
```

```python
import jax
import jax.numpy as jnp
import numpy as np
from jax import lax
from jax.experimental import pallas as pl
from jax.experimental.pallas import tpu as pltpu
from jax.sharding import Mesh, PartitionSpec as P

STATES = 32768
RANGE = 2000
F32, BF16 = jnp.float32, jnp.bfloat16
VM = pl.BlockSpec(memory_space=pltpu.VMEM)
SM = pl.BlockSpec(memory_space=pltpu.SMEM)


SMALL = pl.CostEstimate(flops=1, bytes_accessed=1, transcendentals=0)


def iota(shape, dim):
    return lax.broadcasted_iota(jnp.int32, shape, dim)


def params(mib):
    return pltpu.CompilerParams(vmem_limit_bytes=mib << 20)


def cut_kernel(pos, a, o0, o1, o2, o3):
    for d, o in enumerate((o0, o1, o2, o3)):
        o[...] = a[:, pl.ds(pl.multiple_of(((pos[2] + d) & 3) * 512, 512), 512)]


def cut(pos, a):
    return pl.pallas_call(
        cut_kernel,
        in_specs=[SM, VM],
        out_specs=[VM] * 4,
        out_shape=[jax.ShapeDtypeStruct((128, 512), BF16)] * 4,
        compiler_params=params(8),
        cost_estimate=SMALL,
        name="cut",
    )(pos, a)


def pick_kernel(pos, ids, table, out, slab, sems):
    parts = ((0, 512), (512, 512), (1024, 512), (1536, 464))
    copies = [
        pltpu.make_async_copy(table.at[pl.ds(start, size)], slab.at[pl.ds(start, size)], sems.at[n])
        for n, (start, size) in enumerate(parts)
    ]
    for copy in copies:
        copy.start()
    local = ids[...] - pos[0] * RANGE
    mine = (local >= 0) & (local < RANGE)
    upto = (iota((128, 128), 0) <= iota((128, 128), 1)).astype(BF16)
    count = jnp.dot(mine.astype(F32).astype(BF16), upto, preferred_element_type=F32)
    value = jnp.where(mine, local, 0).astype(F32)
    count = jnp.where(mine, count, 0.0)
    wide = lambda a: jnp.broadcast_to(a[:, None, :], (16, 8, 128)).reshape(128, 128)
    order = ((iota((128, 128), 0) & 7) + 1).astype(F32)
    word = jnp.sum(jnp.where(wide(count) == order, wide(value), 0.0), axis=1, keepdims=True).astype(jnp.int32)
    rows = jnp.zeros((128, 2048), F32)
    for copy, (start, size) in zip(copies, parts):
        hot = (iota((128, size), 1) + start == word).astype(F32).astype(BF16)
        copy.wait()
        rows += jnp.dot(hot, slab[start : start + size, :], preferred_element_type=F32)
    for x in range(4):
        out[:, x] = rows[:, x * 512 : (x + 1) * 512].astype(BF16).reshape(4, 32, 512)


def pick(pos, ids, emission):
    return pl.pallas_call(
        pick_kernel,
        in_specs=[SM, VM, pl.BlockSpec(memory_space=pl.ANY)],
        out_specs=VM,
        out_shape=jax.ShapeDtypeStruct((4, 4, 32, 512), BF16),
        scratch_shapes=[pltpu.VMEM((RANGE, 2048), BF16), pltpu.SemaphoreType.DMA((4,))],
        compiler_params=params(58),
        cost_estimate=SMALL,
        name="pick",
    )(pos, ids, emission)


def moves_kernel(pos, ids, out):
    before = (iota((128, 128), 0) < iota((128, 128), 1)).astype(BF16)
    for block in range(4):
        word = ids[pl.ds(pos[1] * 4 + block, 1), :]
        wordb = jnp.broadcast_to(word, (16, 128))
        owner_at = iota((16, 128), 0)
        owns = (wordb >= owner_at * RANGE) & (wordb < (owner_at + 1) * RANGE)
        ownf = owns.astype(F32)
        earlier = jnp.dot(ownf.astype(BF16), before, preferred_element_type=F32)
        place = ownf * (earlier + (owner_at * 8).astype(F32))
        slot = jnp.sum(place, axis=0, keepdims=True).astype(jnp.int32)
        out[block] = (iota((128, 128), 0) == slot).astype(F32).T.astype(BF16)


def moves(pos, ids):
    return pl.pallas_call(
        moves_kernel,
        in_specs=[SM, VM],
        out_specs=VM,
        out_shape=jax.ShapeDtypeStruct((4, 128, 128), BF16),
        compiler_params=params(8),
        cost_estimate=SMALL,
        name="moves",
    )(pos, ids)


def scale_kernel(pos, move, rows, c0, c1, c2, c3, out, wide):
    wide[...] = rows[...].astype(F32)
    for d, c in enumerate((c0, c1, c2, c3)):
        block = (pos[2] - d + 4) & 3
        given = wide[:, pl.ds(pl.multiple_of(block * 8, 8), 8), :].reshape(128, 512).astype(BF16)
        emitted = jnp.dot(move[block], given, preferred_element_type=F32)
        out[block] = (emitted * c[...].astype(F32)).astype(BF16)


def scale(pos, move, rows, cuts):
    return pl.pallas_call(
        scale_kernel,
        in_specs=[SM] + [VM] * 6,
        out_specs=VM,
        out_shape=jax.ShapeDtypeStruct((4, 128, 512), BF16),
        scratch_shapes=[pltpu.VMEM((16, 32, 512), F32)],
        compiler_params=params(16),
        cost_estimate=pl.CostEstimate(flops=10**10, bytes_accessed=10**7, transcendentals=0),
        name="scale",
    )(pos, move, rows, *cuts)


def quarter(pos, transition, away):
    return transition[:, pl.ds(pl.multiple_of(((pos[2] + away + 4) & 3) * 512, 512), 512)]


def join_kernel(l0, l1, l2, out):
    out[0:1] = l0[...]
    out[1:2] = l1[...]
    out[2:4] = l2[...]


def join(line):
    return pl.pallas_call(
        join_kernel,
        in_specs=[VM] * 3,
        out_specs=VM,
        out_shape=jax.ShapeDtypeStruct((4, 128, 128), BF16),
        compiler_params=params(8),
        cost_estimate=pl.CostEstimate(flops=3 * 10**10, bytes_accessed=10**6, transcendentals=0),
        name="join",
    )(*line)


def pack_kernel(pos, l0, l1, l2, l3, transition, ahead, behind):
    step = 1 - 2 * pos[3]
    near, far, back = (quarter(pos, transition, away) for away in (step, 2, -step))
    for n in range(4):
        lanes = slice(n * 128, (n + 1) * 128)
        ahead[n] = near[:, lanes]
        ahead[12 + n] = far[:, lanes]
        behind[n] = back[:, lanes]
    m = 0
    for part in (l0, l1, l2, l3):
        for n in range(part.shape[0]):
            ahead[4 + m] = part[n]
            behind[4 + m] = part[n]
            m += 1


def pack(pos, line, transition):
    return pl.pallas_call(
        pack_kernel,
        in_specs=[SM] + [VM] * 5,
        out_specs=[VM] * 2,
        out_shape=[jax.ShapeDtypeStruct((16, 128, 128), BF16), jax.ShapeDtypeStruct((12, 128, 128), BF16)],
        compiler_params=params(8),
        cost_estimate=SMALL,
        name="pack",
    )(pos, *line, transition)


def turn_kernel(pos, *refs):
    out = refs[8]
    for c in range(2):
        core = pos[3] ^ c
        step = 1 - 2 * core
        for n, (away, first) in enumerate(((0, 4), (-step, 4 - 4 * c), (step, 4), (2, 0))):
            x = (pos[2] + away + 4) & 3
            for m, flip in enumerate((0, 2, 6, 4, 1, 3, 7, 5)):
                block = (pos[4] ^ flip) * 2 + core
                rows = pl.ds(pl.multiple_of(x * 128, 128), 128)
                times = pl.ds(pl.multiple_of((block & 3) * 128, 128), 128)
                out[block >> 2, rows, times] = refs[c * 4 + n][first + m].T


def turn(pos, parts):
    return pl.pallas_call(
        turn_kernel,
        in_specs=[SM] + [VM] * 8,
        out_specs=VM,
        out_shape=jax.ShapeDtypeStruct((4, 512, 512), BF16),
        compiler_params=params(16),
        cost_estimate=SMALL,
        name="turn",
    )(pos, *parts)


def expect_kernel(pos, alpha, s0, s1, s2, s3, transition, t1, t2, t3, total, sums, e1, e2, e3):
    step = 1 - 2 * pos[3]
    groups = (pos[1], (pos[1] - step + 4) & 3, (pos[1] + step + 4) & 3, (pos[1] + 2) & 3)
    acc = jnp.zeros((512, 512), F32)
    for group, part in zip(groups, (s0, s1, s2, s3)):
        acc += jnp.dot(alpha[group], part[...], preferred_element_type=F32)
    total[...] = acc.reshape(4, 128, 512)
    for d, e in enumerate((e1, e2, e3), 1):
        power = total[(pos[2] + d) & 3]
        power = power * power
        power = power * power
        e[...] = (power * power).astype(BF16)
    for t, first, away in ((None, 0, 0), (t1, 0, -step), (t2, 0, step), (t3, 8, 2)):
        block = (pos[2] + away + 4) & 3
        lanes = jnp.zeros((128, 128), F32)
        if t is None:
            mine = quarter(pos, transition, 0)
        for n in range(4):
            part = slice(n * 128, (n + 1) * 128)
            weight = mine[:, part] if t is None else t[first + n]
            lanes += weight.astype(F32) * total[block, :, part]
        line = jnp.sum(lanes.T, axis=0, keepdims=True)
        sums[pl.ds(block, 1)] = line[None]


def expect(pos, alpha, parts, transition, quarters):
    return pl.pallas_call(
        expect_kernel,
        in_specs=[SM] + [VM] * 9,
        out_specs=[VM] * 5,
        out_shape=[
            jax.ShapeDtypeStruct((4, 128, 512), F32),
            jax.ShapeDtypeStruct((4, 1, 128), F32),
            *[jax.ShapeDtypeStruct((128, 512), BF16)] * 3,
        ],
        compiler_params=params(24),
        cost_estimate=SMALL,
        name="expect",
    )(pos, alpha, *parts, transition, *quarters)


def column_kernel(sums, out):
    whole = jnp.sum(sums[...].reshape(32, 128), axis=0, keepdims=True)
    out[...] = STATES / jnp.broadcast_to(whole, (128, 128)).T


def column(sums):
    return pl.pallas_call(
        column_kernel,
        in_specs=[VM],
        out_specs=VM,
        out_shape=jax.ShapeDtypeStruct((128, 128), F32),
        compiler_params=params(8),
        cost_estimate=pl.CostEstimate(flops=int(2 * 10**9), bytes_accessed=10**6, transcendentals=0),
        name="column",
    )(sums)


def finish_kernel(pos, transition, total, e1, e2, e3, rate, counts, out, kept, rounded, sems):
    copies = []
    for d, e in enumerate((None, e1, e2, e3)):
        part = pl.ds(pl.multiple_of(((pos[2] - d + 4) & 3) * 512, 512), 512)
        if d:
            root = lax.rsqrt(lax.rsqrt(e[...].astype(F32)))
            expected = root * lax.rsqrt(root)
        else:
            expected = total[pos[2]]
        count = transition[:, part].astype(F32) * expected
        kept[d] = count
        rounded[d] = (count * jnp.concatenate([rate[...]] * 4, axis=1)).astype(BF16)
        copies.append(pltpu.make_async_copy(kept.at[d], counts.at[:, part], sems.at[2 * d]))
        copies.append(pltpu.make_async_copy(rounded.at[d], out.at[:, part], sems.at[2 * d + 1]))
        copies[-2].start()
        copies[-1].start()
    for copy in copies:
        copy.wait()


def finish(pos, transition, total, parts, rate):
    return pl.pallas_call(
        finish_kernel,
        in_specs=[SM] + [VM] * 6,
        out_specs=[pl.BlockSpec(memory_space=pl.ANY)] * 2,
        out_shape=[jax.ShapeDtypeStruct((128, 2048), F32), jax.ShapeDtypeStruct((128, 2048), BF16)],
        scratch_shapes=[
            pltpu.VMEM((4, 128, 512), F32),
            pltpu.VMEM((4, 128, 512), BF16),
            pltpu.SemaphoreType.DMA((8,)),
        ],
        compiler_params=params(16),
        cost_estimate=SMALL,
        name="finish",
    )(pos, transition, total, *parts, rate)


def ring(step, size=4):
    return [(i, (i + step) % size) for i in range(size)]


def per_device(ids, alpha, beta, emission, transition):
    y, x, z, k = (lax.axis_index(a) for a in ("y", "x", "z", "k"))
    pos = jnp.stack([y * 4 + x, y, x, k, z]).astype(jnp.int32)
    ids = ids.reshape(16, 128)
    ahead = [(a * 2 + c, ((a + 1 - 2 * c) % 4) * 2 + c) for a in range(4) for c in range(2)]
    behind = [(b, a) for a, b in ahead]
    swap = [(0, 1), (1, 0)]

    together = lax.optimization_barrier
    flip = lambda a, by: lax.ppermute(a, "z", [(i, i ^ by) for i in range(8)])

    line = [alpha[None], flip(alpha[None], 2)]
    betas = [c if d == 0 else lax.ppermute(c, "x", ring(d)) for d, c in enumerate(cut(pos, beta))]
    picked = pick(pos, ids, emission)
    picked, line, betas = together((picked, line, betas))

    rows = lax.all_to_all(picked.reshape(16, 32, 512), ("y", "x"), 0, 0)
    line.append(flip(jnp.concatenate(line), 6))
    line.append(flip(join(line), 1))
    ids, _ = together((ids, line[2]))
    own = scale(pos, moves(pos, ids), rows, betas).reshape(512, 512)

    one = lax.ppermute(own, ("y", "k"), ahead)
    two = lax.ppermute(own, ("y", "k"), behind)
    to_a, to_b = pack(pos, line, transition)
    one_a = lax.ppermute(to_a, ("x", "k"), ahead)
    later, one_a = together((to_b, one_a))
    two_a = lax.ppermute(later, ("x", "k"), behind)

    far = lax.ppermute(one, ("y", "k"), ahead)
    one_c = one_a[4:]
    far_a = lax.ppermute(one_c, ("x", "k"), ahead)
    one_c, far_a, two = together((one_c, far_a, two))
    sources = [to_b, one_a, two_a, far_a]
    sources += [lax.ppermute(a, "k", swap) for a in (to_b, one_c, two_a, far_a)]
    alpha_t = turn(pos, sources)

    total, sums, *parts = expect(pos, alpha_t, (own, one, two, far), transition, (one_a, two_a, far_a))
    sums = sums + lax.ppermute(sums, "k", swap)
    sums = jnp.broadcast_to(sums[None], (8, 4, 1, 128)).reshape(32, 1, 128)
    sums = lax.all_to_all(sums, ("z", "x"), 0, 0)
    parts = [lax.ppermute(e, "x", ring(d)) for d, e in enumerate(parts, 1)]
    return finish(pos, transition, total, parts, column(sums))


def solution(mesh):
    fine = Mesh(np.asarray(mesh.devices).reshape(4, 4, 8, 2), ("y", "x", "z", "k"))
    row, col = ("y", "x"), ("z", "k")
    in_specs = (P(), P(col, row), P(row, col), P(row, col), P(row, col))
    out_specs = (P(row, col), P(row, col))
    return jax.shard_map(per_device, mesh=fine, in_specs=in_specs, out_specs=out_specs, check_vma=False)
```
